512 devices in a mesh: energy: 64 (over x, y_hi, z), slab: 8 (over y_lo, core).
Axes of the slice: x: 4, y: 8 (y_hi: 2, y_lo: 4; y = y_hi * 4 + y_lo), z: 8, core: 2. Of those that a mesh axis runs over, the one named last changes fastest.
Arguments:
- green0: bfloat16 [64, 8, 2, 384, 384], P('energy', 'slab'), may hold values from -6 to 6
- coupling: bfloat16 [8, 3, 384, 384], P('slab'), may hold values from -0.09375 to 0.09375
Outputs:
- green: bfloat16 [64, 8, 2, 384, 384], P('energy', 'slab')
The draws below stay inside these ranges and needn't reach their ends.
All inputs are finite; a program needn't handle non-finite values.
Results may differ from the reference program's by a relative error of at most 0.012.
Values may be sent and summed in bfloat16 or wider, within the bound.
A program may use at most 64 MiB of HBM per device.

```python
import jax
import jax.numpy as jnp
from jax import lax

B = 384
OFFSET = 7
ITERS = 2
ENERGIES = 64
SLABS = 8


def levels(own_key, dims, cuts, smallest, high):
    def one(axis_at, shards_of):
        heights = jax.random.uniform(jax.random.fold_in(jax.random.fold_in(own_key, 6), axis_at), (shards_of,), jnp.float32, smallest / len(cuts), high / len(cuts))
        return jnp.repeat(jnp.exp(heights), dims[axis_at] // shards_of).reshape((-1,) + (1,) * (len(dims) - axis_at - 1))

    level = one(*cuts[0])
    for cut in cuts[1:]:
        level = level * one(*cut)
    return level


def bell_draw(key, extent, width, most, cuts=(), held_as=jnp.bfloat16):
    drawn = width * jax.random.normal(key, extent, jnp.float32)
    if cuts:
        drawn = drawn * levels(key, extent, cuts, -0.22, 0.18)
    return jnp.clip(drawn, -most, most).astype(held_as)


def setup_inputs(seed: int = 0) -> dict:
    key_of = jax.random.split(jax.random.key(seed), 3)
    return {
        "green0": bell_draw(key_of[0], (ENERGIES, SLABS, 2, B, B), 1.0, 6.0, ((0, 64), (1, 8))),
        "coupling": bell_draw(key_of[1], (SLABS, 3, B, B), (10 * B) ** -0.5, 0.09375, ((0, 8),)),
    }


def mult(form, left, right):
    return jnp.einsum(form, left.astype(jnp.float32), right.astype(jnp.float32), precision=lax.Precision.HIGHEST)


def dyson(green0, coupling, summed):
    count = green0.shape[0]
    sigma = jnp.zeros(green0.shape, jnp.float32)
    for index in range(3):
        part = summed[index:index + count]
        weights = coupling[:, index]
        left = mult("sij,scjk->scik", weights, part).astype(jnp.bfloat16)
        sigma = sigma + mult("scij,skj->scik", left, weights)
    sigma = sigma.astype(jnp.bfloat16)
    green_re = green0[:, 0]
    green_im = green0[:, 1]
    prod_re = mult("sij,sjk->sik", green_re, sigma[:, 0]) - mult("sij,sjk->sik", green_im, sigma[:, 1])
    prod_im = mult("sij,sjk->sik", green_re, sigma[:, 1]) + mult("sij,sjk->sik", green_im, sigma[:, 0])
    prod_re = prod_re.astype(jnp.bfloat16)
    prod_im = prod_im.astype(jnp.bfloat16)
    out_re = mult("sij,skj->sik", prod_re, green_re) - mult("sij,skj->sik", prod_im, green_im)
    out_im = mult("sij,skj->sik", prod_re, green_im) + mult("sij,skj->sik", prod_im, green_re)
    result = green0.astype(jnp.float32) + jnp.stack([out_re, out_im], axis=1) / B
    return result.astype(jnp.bfloat16)


def reference(green0, coupling):
    green = green0
    for turn in range(ITERS):
        empty = jnp.zeros((OFFSET,) + green.shape[1:], jnp.bfloat16)
        lower = jnp.concatenate([empty, green[:-OFFSET]], axis=0)
        upper = jnp.concatenate([green[OFFSET:], empty], axis=0)
        both = (lower.astype(jnp.float32) + upper.astype(jnp.float32)).astype(jnp.bfloat16)
        summed = jnp.pad(both, ((0, 0), (1, 1), (0, 0), (0, 0), (0, 0)))
        green = lax.map(lambda pair: dyson(pair[0], coupling, pair[1]), (green0, summed))
    return green
```

```python
import functools

import jax
import jax.numpy as jnp
from jax import lax
from jax.experimental import pallas as pl
from jax.experimental.pallas import tpu as pltpu
from jax.sharding import PartitionSpec as P

MESH = pl.DeviceIdType.MESH
B = 384
N = 3
R = B // N
BF = jnp.bfloat16
F32 = jnp.float32
NT = (((1,), (1,)), ((), ()))
SWAP, LOW, HIGH, WRAP, SIDE, HALO, VLOW, VHIGH, HALO2 = 0, 1, 2, 3, 4, 5, 9, 10, 11
KINDS = 13


def dot(a, b):
    return jnp.dot(a, b, preferred_element_type=F32)


def dot_nt(a, b):
    return lax.dot_general(a, b, NT, preferred_element_type=F32)


def kernel(
    g_in, c_in, out,
    base, recv, both, green, vrecv, both2, coup, ccat, rights, acc, sig, wide, outbuf,
    send_sem, recv_sem, local_sem,
):
    energy = lax.axis_index("energy")
    s = lax.axis_index("slab")
    g, z = energy // 8, energy % 8
    odd = g % 2
    mirror = g + 1 - 2 * odd
    lower_pair = g - 2 * (1 - odd)
    upper_pair = g + 2 * odd
    first, last = z == 0, z == 7
    edge = first | last
    inner = (z > 0) & (z < 7)
    zu, zd = (z + 1) % 8, (z + 7) % 8
    rows = [pl.ds(c * R, R) for c in range(N)]

    def at(gg, zz):
        return (gg * 8 + zz, s)

    home = (energy, s)
    up = (at(jnp.where(last, g, lower_pair), zu), last | (g >= 1))
    down = (at(jnp.where(first, g, upper_pair), zd), first | (g <= 6))
    vup = (at(jnp.where(last, g, mirror - 1), zu), last | (g != 1))
    vdown = (at(jnp.where(first, g, mirror + 1), zd), first | (g != 6))
    low_from = (at(jnp.where(first, g, mirror + 1), zd), first | (g != 6))
    high_from = (at(jnp.where(last, g, mirror - 1), zu), last | (g != 1))
    vlow_from = (at(jnp.where(first, g, upper_pair), zd), first | (g <= 6))
    vhigh_from = (at(jnp.where(last, g, lower_pair), zu), last | (g >= 1))
    slab_low, slab_high = (energy, s - 1), (energy, s + 1)
    side_in = (first & (g >= 1)) | (last & (g <= 6))
    side_out = ((z == 1) & (g != 6)) | ((z == 6) & (g != 1))

    def remote(kind, c, src, dst, dev):
        return pltpu.make_async_remote_copy(
            src_ref=src.at[rows[c]], dst_ref=dst.at[rows[c]],
            send_sem=send_sem.at[kind, c], recv_sem=recv_sem.at[kind, c],
            device_id=dev, device_id_type=MESH,
        )

    def start(kind, c, src, dst, dev, cond):
        @pl.when(cond)
        def _():
            remote(kind, c, src, dst, dev).start()

    def arrived(kind, c, dst, cond):
        @pl.when(cond)
        def _():
            remote(kind, c, dst, dst, home).wait_recv()

    def sent(kind, c, src, cond):
        @pl.when(cond)
        def _():
            remote(kind, c, src, src, home).wait_send()

    true = s >= 0
    mir, own = base.at[0], base.at[1]

    loads = [
        pltpu.make_async_copy(g_in.at[0], base.at[1, :, pl.ds(0, B)], local_sem.at[0]),
        pltpu.make_async_copy(g_in.at[1], base.at[1, :, pl.ds(B, B)], local_sem.at[1]),
        pltpu.make_async_copy(c_in, coup, local_sem.at[2]),
    ]
    for load in loads:
        load.start()

    barrier = pltpu.get_barrier_semaphore()
    pl.semaphore_signal(barrier, inc=1, device_id=at(mirror, z), device_id_type=MESH)
    count = jnp.int32(1)
    for dev, cond in (low_from, high_from, vlow_from, vhigh_from, (slab_low, s >= 1), (slab_high, s <= 6)):
        @pl.when(cond)
        def _(dev=dev):
            pl.semaphore_signal(barrier, inc=1, device_id=dev, device_id_type=MESH)
    for cond in (up[1], down[1], vup[1], vdown[1], s >= 1, s <= 6):
        count = count + cond.astype(jnp.int32)
    loads[0].wait()
    loads[1].wait()
    pl.semaphore_wait(barrier, count)

    for c in range(N):
        start(SWAP, c, own, mir, at(mirror, z), true)
        start(LOW, c, own, recv.at[0], *up)
        start(HIGH, c, own, recv.at[1], *down)

    def clear(ref, cond):
        @pl.when(cond)
        def _():
            ref[...] = jnp.zeros(ref.shape, ref.dtype)

    clear(recv.at[0], ~low_from[1])
    clear(recv.at[1], ~high_from[1])
    clear(recv.at[3], edge & ~side_in)
    clear(vrecv.at[0], ~vlow_from[1])
    clear(vrecv.at[1], ~vhigh_from[1])
    for target in (both.at[0], both.at[1], both2):
        clear(target.at[0], s == 0)
        clear(target.at[2], s == 7)

    loads[2].wait()
    for c in range(N):
        for k in range(3):
            ccat[c, :, k * R : (k + 1) * R] = coup[k, :, c * R : (c + 1) * R]

    def widen(j, c):
        re = base[j, rows[c], 0:B]
        im = base[j, rows[c], B : 2 * B]
        wide[j, pl.ds(c * R, R), 0:B] = re
        wide[j, pl.ds(c * R, R), B : 2 * B] = -im
        wide[j, pl.ds(B + c * R, R), 0:B] = im
        wide[j, pl.ds(B + c * R, R), B : 2 * B] = re

    for c in range(N):
        widen(1, c)

    def add_up(target, a, b, c):
        target[1, rows[c]] = (a[rows[c]].astype(F32) + b[rows[c]].astype(F32)).astype(BF)

    def pass_halo(kind, c, target):
        start(kind, c, target.at[1], target.at[2], slab_low, s >= 1)
        start(kind + 1, c, target.at[1], target.at[0], slab_high, s <= 6)

    def await_halo(kind, c, target, cond):
        arrived(kind, c, target.at[2], cond & (s <= 6))
        arrived(kind + 1, c, target.at[0], cond & (s >= 1))

    def sigma_part(target, c, to):
        for k in range(3):
            stacked = jnp.concatenate([target[k, rows[c], 0:B], target[k, rows[c], B : 2 * B]], axis=0)
            right = dot_nt(stacked, coup[k]).astype(BF)
            rights[k * R : (k + 1) * R, 0:B] = right[0:R]
            rights[k * R : (k + 1) * R, B : 2 * B] = right[R : 2 * R]
        part = dot(ccat[c], rights[...])
        if c == 0:
            to[...] = part
        else:
            to[...] += part

    def round_sigma(total):
        re = total[:, 0:B].astype(BF)
        im = total[:, B : 2 * B].astype(BF)
        sig[0:B, 0:B] = re
        sig[0:B, B : 2 * B] = im
        sig[B : 2 * B, 0:B] = -im
        sig[B : 2 * B, B : 2 * B] = re

    def result(j, c):
        here = base[j, rows[c]]
        prod = dot(here, sig[...]).astype(BF)
        return here.astype(F32) + dot_nt(prod, wide[j]) * (1.0 / B)

    for c in range(N):
        @pl.when(inner)
        def _(c=c):
            arrived(LOW, c, recv.at[0], low_from[1])
            arrived(HIGH, c, recv.at[1], high_from[1])
            add_up(both.at[0], recv.at[0], recv.at[1], c)
            pass_halo(HALO, c, both.at[0])

    for c in range(N):
        arrived(SWAP, c, mir, true)
        start(WRAP, c, mir, recv.at[2], at(g, jnp.where(first, 7, 0)), edge)
        start(SIDE, c, mir, recv.at[3],
              at(jnp.where(z == 1, mirror + 1, mirror - 1), jnp.where(z == 1, 0, 7)), side_out)
        widen(0, c)

        @pl.when(inner)
        def _(c=c):
            await_halo(HALO, c, both.at[0], true)
            sigma_part(both.at[0], c, acc.at[0])

    @pl.when(edge)
    def _():
        a0, b0 = jnp.where(first, 2, 0), jnp.where(last, 2, 1)
        a1, b1 = jnp.where(first, 0, 3), jnp.where(first, 3, 1)
        for c in range(N):
            arrived(LOW, c, recv.at[0], low_from[1])
            arrived(HIGH, c, recv.at[1], high_from[1])
            arrived(WRAP, c, recv.at[2], true)
            add_up(both.at[0], recv.at[a0], recv.at[b0], c)
            pass_halo(HALO, c, both.at[0])
            arrived(SIDE, c, recv.at[3], side_in)
            add_up(both.at[1], recv.at[a1], recv.at[b1], c)
            pass_halo(HALO + 2, c, both.at[1])
        for c in range(N):
            for j in range(2):
                await_halo(HALO + 2 * j, c, both.at[j], true)
                sigma_part(both.at[j], c, acc.at[j])

    round_sigma(acc.at[0])
    for c in range(N):
        green[0, rows[c]] = result(0, c).astype(BF)
        start(VLOW, c, green.at[0], vrecv.at[0], vup[0], vup[1] & ~last)
        start(VHIGH, c, green.at[0], vrecv.at[1], vdown[0], vdown[1] & ~first)

    @pl.when(edge)
    def _():
        round_sigma(acc.at[1])
        for c in range(N):
            green[1, rows[c]] = result(1, c).astype(BF)
            start(VLOW, c, green.at[1], vrecv.at[0], vup[0], last)
            start(VHIGH, c, green.at[1], vrecv.at[1], vdown[0], first)

    for c in range(N + 1):
        if c < N:
            arrived(VLOW, c, vrecv.at[0], vlow_from[1])
            arrived(VHIGH, c, vrecv.at[1], vhigh_from[1])
            add_up(both2, vrecv.at[0], vrecv.at[1], c)
            pass_halo(HALO2, c, both2)
        if c > 0:
            await_halo(HALO2, c - 1, both2, true)
            sigma_part(both2, c - 1, acc.at[0])
    round_sigma(acc.at[0])
    stores = []
    for c in range(N):
        outbuf[rows[c]] = result(1, c).astype(BF)
        for part in range(2):
            store = pltpu.make_async_copy(
                outbuf.at[rows[c], pl.ds(part * B, B)], out.at[part, rows[c]], local_sem.at[3 + 2 * c + part]
            )
            store.start()
            stores.append(store)

    for c in range(N):
        sent(SWAP, c, own, true)
        sent(LOW, c, own, up[1])
        sent(HIGH, c, own, down[1])
        sent(WRAP, c, mir, edge)
        sent(SIDE, c, mir, side_out)
        for j in range(2):
            cond = true if j == 0 else edge
            sent(HALO + 2 * j, c, both.at[j, 1], cond & (s >= 1))
            sent(HALO + 2 * j + 1, c, both.at[j, 1], cond & (s <= 6))
        sent(VLOW, c, green.at[0], vup[1])
        sent(VHIGH, c, green.at[0], vdown[1])
        sent(HALO2, c, both2.at[1], s >= 1)
        sent(HALO2 + 1, c, both2.at[1], s <= 6)
    for store in stores:
        store.wait()


def local(green0, coupling):
    block = (B, 2 * B)
    result = pl.pallas_call(
        kernel,
        out_shape=jax.ShapeDtypeStruct((2, B, B), BF),
        in_specs=[pl.BlockSpec(memory_space=pl.ANY)] * 2,
        out_specs=pl.BlockSpec(memory_space=pl.ANY),
        scratch_shapes=[
            pltpu.VMEM((2, *block), BF),
            pltpu.VMEM((4, *block), BF),
            pltpu.VMEM((2, 3, *block), BF),
            pltpu.VMEM((2, *block), BF),
            pltpu.VMEM((2, *block), BF),
            pltpu.VMEM((3, *block), BF),
            pltpu.VMEM((3, B, B), BF),
            pltpu.VMEM((N, B, 3 * R), BF),
            pltpu.VMEM((3 * R, 2 * B), BF),
            pltpu.VMEM((2, *block), F32),
            pltpu.VMEM((2 * B, 2 * B), BF),
            pltpu.VMEM((2, 2 * B, 2 * B), BF),
            pltpu.VMEM(block, BF),
            pltpu.SemaphoreType.DMA((KINDS, N)),
            pltpu.SemaphoreType.DMA((KINDS, N)),
            pltpu.SemaphoreType.DMA((3 + 2 * N,)),
        ],
        compiler_params=pltpu.CompilerParams(
            collective_id=0, has_side_effects=True, vmem_limit_bytes=48 * 1024 * 1024
        ),
        name="born",
    )(green0[0, 0], coupling[0])
    return result[None, None]


def solution(mesh):
    return jax.shard_map(
        local,
        mesh=mesh,
        in_specs=(P("energy", "slab", None, None, None), P("slab", None, None, None)),
        out_specs=P("energy", "slab", None, None, None),
        check_vma=False,
    )
```

```python
import functools

import jax
import jax.numpy as jnp
from jax import lax
from jax.experimental import pallas as pl
from jax.experimental.pallas import tpu as pltpu
from jax.sharding import PartitionSpec as P

MESH = pl.DeviceIdType.MESH
B = 384
N = 6
R = B // N
NC = 3
RC = B // NC
PER = N // NC
WINDOW = 3
NL = 3
LAG, LAG1, LAG2 = 2, 1, 2
BF = jnp.bfloat16
F32 = jnp.float32
NT = (((1,), (1,)), ((), ()))
SWAP, LOW, HIGH, WRAP, SIDE, HALO, VLOW, VHIGH, HALO2 = 0, 1, 2, 3, 4, 5, 9, 10, 11
RELAY, ONWARD = 13, 14
KINDS = 15
DETOURS = ((0, 4, 2), (0, 5, 3), (1, 5, 2))


def dot(a, b):
    return jnp.dot(a, b, preferred_element_type=F32)


def dot_nt(a, b):
    return lax.dot_general(a, b, NT, preferred_element_type=F32)


def kernel(
    g_in, c_in, out,
    base, recv, passing, both, green, vrecv, both2, coup, ccat, rights, acc, sig, wide,
    send_sem, recv_sem, local_sem,
):
    energy = lax.axis_index("energy")
    s = lax.axis_index("slab")
    g, z = energy // 8, energy % 8
    odd = g % 2
    mirror = g + 1 - 2 * odd
    lower_pair = g - 2 * (1 - odd)
    upper_pair = g + 2 * odd
    first, last = z == 0, z == 7
    edge = first | last
    zu, zd = (z + 1) % 8, (z + 7) % 8
    rows = [pl.ds(c * R, R) for c in range(N)]
    thick = [pl.ds(c * (B // NL), B // NL) for c in range(NL)]

    def piece(kind, c):
        return thick[c] if kind in (LOW, HIGH) else rows[c]

    def at(gg, zz):
        return (gg * 8 + zz, s)

    home = (energy, s)
    true = s >= 0
    up = (at(jnp.where(last, g, lower_pair), zu), last | (g >= 1))
    down = (at(jnp.where(first, g, upper_pair), zd), first | (g <= 6))
    vup = (at(jnp.where(last, g, mirror - 1), zu), last | (g != 1))
    vdown = (at(jnp.where(first, g, mirror + 1), zd), first | (g != 6))
    side_out = ((z == 1) & (g != 6)) | ((z == 6) & (g != 1))
    across = at(mirror, z)
    side_to = at(jnp.where(z == 1, mirror + 1, mirror - 1), jnp.where(z == 1, 0, 7))
    opposite = at(g, jnp.where(first, 7, 0))
    low_from = (at(jnp.where(first, g, mirror + 1), zd), first | (g != 6))
    high_from = (at(jnp.where(last, g, mirror - 1), zu), last | (g != 1))
    vlow_from = (at(jnp.where(first, g, upper_pair), zd), first | (g <= 6))
    vhigh_from = (at(jnp.where(last, g, lower_pair), zu), last | (g >= 1))
    slab_low, slab_high = ((energy, s - 1), s >= 1), ((energy, s + 1), s <= 6)
    side_in = (first & (g >= 1)) | (last & (g <= 6))

    def remote(kind, c, src, dst, dev, arrives):
        return pltpu.make_async_remote_copy(
            src_ref=src.at[piece(kind, c)], dst_ref=dst.at[piece(kind, c)],
            send_sem=send_sem.at[kind, c], recv_sem=recv_sem.at[arrives, c],
            device_id=dev, device_id_type=MESH,
        )

    def start(kind, c, src, dst, dev, cond, arrives=None):
        @pl.when(cond)
        def _():
            remote(kind, c, src, dst, dev, kind if arrives is None else arrives).start()

    def arrived(kind, c, dst, cond):
        @pl.when(cond)
        def _():
            remote(kind, c, dst, dst, home, kind).wait_recv()

    def sent(kind, c, src, cond):
        @pl.when(cond)
        def _():
            remote(kind, c, src, src, home, kind).wait_send()

    mir, own = base.at[0], base.at[1]

    loads = [
        pltpu.make_async_copy(g_in.at[0], base.at[1, :, pl.ds(0, B)], local_sem.at[0]),
        pltpu.make_async_copy(g_in.at[1], base.at[1, :, pl.ds(B, B)], local_sem.at[1]),
        pltpu.make_async_copy(c_in, coup, local_sem.at[2]),
    ]
    for load in loads:
        load.start()

    def flipped(zz):
        return jnp.where(z < 4, zz, 7 - zz)

    barrier = pltpu.get_barrier_semaphore()
    count = jnp.int32(1)
    for dev, cond in (
        low_from, high_from, vlow_from, vhigh_from, slab_low, slab_high,
        (across, true),
        *((at(g, flipped(source)), z == flipped(relay)) for source, _, relay in DETOURS),
        *((at(mirror, flipped(relay)), z == flipped(source)) for source, _, relay in DETOURS),
    ):
        @pl.when(cond)
        def _(dev=dev):
            pl.semaphore_signal(barrier, inc=1, device_id=dev, device_id_type=MESH)
    for cond in (
        up[1], down[1], vup[1], vdown[1], slab_low[1], slab_high[1],
        *(z == flipped(source) for source, _, _ in DETOURS),
        *(z == flipped(relay) for _, _, relay in DETOURS),
    ):
        count = count + cond.astype(jnp.int32)
    loads[0].wait()
    loads[1].wait()
    pl.semaphore_wait(barrier, count)

    def direct(c):
        cond = true
        for source, piece, _ in DETOURS:
            if piece == c:
                cond = cond & (z != flipped(source))
        return cond

    def detour(i):
        source, piece, relay = DETOURS[i]
        return pltpu.make_async_remote_copy(
            src_ref=own.at[rows[piece]], dst_ref=passing.at[i],
            send_sem=send_sem.at[RELAY, i], recv_sem=recv_sem.at[RELAY, i],
            device_id=at(g, flipped(relay)), device_id_type=MESH,
        )

    def onward(i):
        source, piece, relay = DETOURS[i]
        return pltpu.make_async_remote_copy(
            src_ref=passing.at[i], dst_ref=mir.at[rows[piece]],
            send_sem=send_sem.at[ONWARD, i], recv_sem=recv_sem.at[SWAP, piece],
            device_id=at(mirror, flipped(source)), device_id_type=MESH,
        )

    def swap(c):
        start(SWAP, c, own, mir, across, direct(c))

    for i, (source, _, _) in enumerate(DETOURS):
        @pl.when(z == flipped(source))
        def _(i=i):
            detour(i).start()
    for c in range(N):
        if c < WINDOW:
            swap(c)
        if c < NL:
            start(LOW, c, own, recv.at[0], *up)
            start(HIGH, c, own, recv.at[1], *down)

    def clear(ref, cond):
        @pl.when(cond)
        def _():
            ref[...] = jnp.zeros(ref.shape, ref.dtype)

    clear(recv.at[0], ~low_from[1])
    clear(recv.at[1], ~high_from[1])
    clear(recv.at[3], edge & ~side_in)
    clear(vrecv.at[0], ~vlow_from[1])
    clear(vrecv.at[1], ~vhigh_from[1])
    for target in (both.at[0], both.at[1], both2):
        clear(target.at[0], s == 0)
        clear(target.at[2], s == 7)

    loads[2].wait()
    for c in range(NC):
        for k in range(3):
            ccat[c, :, k * RC : (k + 1) * RC] = coup[k, :, c * RC : (c + 1) * RC]

    def widen(j, c):
        re = base[j, rows[c], 0:B]
        im = base[j, rows[c], B : 2 * B]
        wide[j, pl.ds(c * R, R), 0:B] = re
        wide[j, pl.ds(c * R, R), B : 2 * B] = -im
        wide[j, pl.ds(B + c * R, R), 0:B] = im
        wide[j, pl.ds(B + c * R, R), B : 2 * B] = re

    for c in range(N):
        widen(1, c)

    def add_up(target, a, b, c):
        target[1, rows[c]] = (a[rows[c]].astype(F32) + b[rows[c]].astype(F32)).astype(BF)

    def pass_halo(kind, c, target, cond=true):
        start(kind, c, target.at[1], target.at[2], slab_low[0], cond & slab_low[1])
        start(kind + 1, c, target.at[1], target.at[0], slab_high[0], cond & slab_high[1])

    def await_halo(kind, c, target):
        arrived(kind, c, target.at[2], slab_high[1])
        arrived(kind + 1, c, target.at[0], slab_low[1])

    def sigma_part(target, c, to):
        here = pl.ds(c * RC, RC)
        for k in range(3):
            stacked = jnp.concatenate([target[k, here, 0:B], target[k, here, B : 2 * B]], axis=0)
            right = dot_nt(stacked, coup[k]).astype(BF)
            rights[k * RC : (k + 1) * RC, 0:B] = right[0:RC]
            rights[k * RC : (k + 1) * RC, B : 2 * B] = right[RC : 2 * RC]
        part = dot(ccat[c], rights[...])
        if c == 0:
            to[...] = part
        else:
            to[...] += part

    def round_sigma(j):
        re = acc[j, :, 0:B].astype(BF)
        im = acc[j, :, B : 2 * B].astype(BF)
        sig[j, 0:B, 0:B] = re
        sig[j, 0:B, B : 2 * B] = im
        sig[j, B : 2 * B, 0:B] = -im
        sig[j, B : 2 * B, B : 2 * B] = re

    def result(j, c):
        here = base[j, pl.ds(c * RC, RC)]
        prod = dot(here, sig[j]).astype(BF)
        return here.astype(F32) + dot_nt(prod, wide[j]) * (1.0 / B)

    def next_swap(c):
        if c + WINDOW < N:
            sent(SWAP, c, own, direct(c))
            swap(c + WINDOW)

    def forward(c):
        arrived(SWAP, c, mir, true)
        next_swap(c)

    for i, (_, _, relay) in enumerate(DETOURS):
        @pl.when(z == flipped(relay))
        def _(i=i):
            detour(i).wait_recv()
            onward(i).start()

    @pl.when(~edge)
    def _():
        for c in range(N + LAG):
            if c < N:
                if c % (N // NL) == 0:
                    arrived(LOW, c // (N // NL), recv.at[0], low_from[1])
                    arrived(HIGH, c // (N // NL), recv.at[1], high_from[1])
                add_up(both.at[0], recv.at[0], recv.at[1], c)
                pass_halo(HALO, c, both.at[0])
                forward(c)
                start(SIDE, c, mir, recv.at[3], side_to, side_out)
                widen(0, c)
            d = c - LAG
            if d >= 0:
                await_halo(HALO, d, both.at[0])
                if d % PER == PER - 1:
                    sigma_part(both.at[0], d // PER, acc.at[0])

    @pl.when(edge)
    def _():
        a0, b0 = jnp.where(first, 2, 0), jnp.where(last, 2, 1)
        a1, b1 = jnp.where(first, 0, 3), jnp.where(first, 3, 1)
        for c in range(N + LAG2):
            if c < N:
                forward(c)
                start(WRAP, c, mir, recv.at[2], opposite, true)
                widen(0, c)
            d = c - LAG1
            if 0 <= d < N:
                if d % (N // NL) == 0:
                    arrived(LOW, d // (N // NL), recv.at[0], low_from[1])
                    arrived(HIGH, d // (N // NL), recv.at[1], high_from[1])
                arrived(WRAP, d, recv.at[2], true)
                add_up(both.at[0], recv.at[a0], recv.at[b0], d)
                pass_halo(HALO, d, both.at[0])
                arrived(SIDE, d, recv.at[3], side_in)
                add_up(both.at[1], recv.at[a1], recv.at[b1], d)
                pass_halo(HALO + 2, d, both.at[1])
            d = c - LAG2
            if d >= 0:
                for j in range(2):
                    await_halo(HALO + 2 * j, d, both.at[j])
                    if d % PER == PER - 1:
                        sigma_part(both.at[j], d // PER, acc.at[j])
        round_sigma(1)

    round_sigma(0)
    for c in range(NC):
        @pl.when(edge)
        def _(c=c):
            green[1, pl.ds(c * RC, RC)] = result(1, c).astype(BF)
            for d in range(c * PER, c * PER + PER):
                start(VLOW, d, green.at[1], vrecv.at[0], vup[0], last)
                start(VHIGH, d, green.at[1], vrecv.at[1], vdown[0], first)
        green[0, pl.ds(c * RC, RC)] = result(0, c).astype(BF)
        for d in range(c * PER, c * PER + PER):
            start(VLOW, d, green.at[0], vrecv.at[0], vup[0], vup[1] & ~last)
            start(VHIGH, d, green.at[0], vrecv.at[1], vdown[0], vdown[1] & ~first)

    for c in range(N + PER):
        if c < N:
            arrived(VLOW, c, vrecv.at[0], vlow_from[1])
            arrived(VHIGH, c, vrecv.at[1], vhigh_from[1])
            add_up(both2, vrecv.at[0], vrecv.at[1], c)
            pass_halo(HALO2, c, both2)
        d = c - PER
        if d >= 0:
            await_halo(HALO2, d, both2)
            if d % PER == PER - 1:
                sigma_part(both2, d // PER, acc.at[1])
    round_sigma(1)
    for c in range(NC):
        here = pl.ds(c * RC, RC)
        final = result(1, c).astype(BF)
        for part in range(2):
            out[part, here] = final[:, part * B : part * B + B]

    for c in range(N):
        if c + WINDOW >= N:
            sent(SWAP, c, own, direct(c))
        if c < NL:
            sent(LOW, c, own, up[1])
            sent(HIGH, c, own, down[1])
        sent(WRAP, c, mir, edge)
        sent(SIDE, c, mir, side_out)
        for j in range(2):
            cond = true if j == 0 else edge
            sent(HALO + 2 * j, c, both.at[j, 1], cond & slab_low[1])
            sent(HALO + 2 * j + 1, c, both.at[j, 1], cond & slab_high[1])
        sent(VLOW, c, green.at[0], vup[1])
        sent(VHIGH, c, green.at[0], vdown[1])
        sent(HALO2, c, both2.at[1], slab_low[1])
        sent(HALO2 + 1, c, both2.at[1], slab_high[1])
    for i, (source, _, relay) in enumerate(DETOURS):
        @pl.when(z == flipped(source))
        def _(i=i):
            detour(i).wait_send()

        @pl.when(z == flipped(relay))
        def _(i=i):
            onward(i).wait_send()


def local(green0, coupling):
    block = (B, 2 * B)
    result = pl.pallas_call(
        kernel,
        out_shape=jax.ShapeDtypeStruct((2, B, B), BF),
        in_specs=[pl.BlockSpec(memory_space=pltpu.HBM)] * 2,
        out_specs=pl.BlockSpec(memory_space=pltpu.VMEM),
        scratch_shapes=[
            pltpu.VMEM((2, *block), BF),
            pltpu.VMEM((4, *block), BF),
            pltpu.VMEM((len(DETOURS), R, 2 * B), BF),
            pltpu.VMEM((2, 3, *block), BF),
            pltpu.VMEM((2, *block), BF),
            pltpu.VMEM((2, *block), BF),
            pltpu.VMEM((3, *block), BF),
            pltpu.VMEM((3, B, B), BF),
            pltpu.VMEM((NC, B, 3 * RC), BF),
            pltpu.VMEM((3 * RC, 2 * B), BF),
            pltpu.VMEM((2, *block), F32),
            pltpu.VMEM((2, 2 * B, 2 * B), BF),
            pltpu.VMEM((2, 2 * B, 2 * B), BF),
            pltpu.SemaphoreType.DMA((KINDS, N)),
            pltpu.SemaphoreType.DMA((KINDS, N)),
            pltpu.SemaphoreType.DMA((3,)),
        ],
        compiler_params=pltpu.CompilerParams(
            collective_id=0, has_side_effects=True, vmem_limit_bytes=53 * 1024 * 1024
        ),
        name="born",
    )(green0[0, 0], coupling[0])
    return result[None, None]


def solution(mesh):
    return jax.shard_map(
        local,
        mesh=mesh,
        in_specs=(P("energy", "slab", None, None, None), P("slab", None, None, None)),
        out_specs=P("energy", "slab", None, None, None),
        check_vma=False,
    )
```

```python
import functools

import jax
import jax.numpy as jnp
from jax import lax
from jax.experimental import pallas as pl
from jax.experimental.pallas import tpu as pltpu
from jax.sharding import PartitionSpec as P

MESH = pl.DeviceIdType.MESH
B = 384
N = 6
R = B // N
NC = 3
RC = B // NC
PER = N // NC
WINDOW = 3
NL = 3
LAG, LAG1, LAG2 = 2, 2, 3
BF = jnp.bfloat16
F32 = jnp.float32
NT = (((1,), (1,)), ((), ()))
SWAP, LOW, HIGH, WRAP, SIDE, HALO, VLOW, VHIGH, HALO2 = 0, 1, 2, 3, 4, 5, 9, 10, 11
RELAY, ONWARD = 13, 14
KINDS = 15
DETOURS = ((0, 4, 2), (0, 5, 3), (1, 5, 2))


def dot(a, b):
    return jnp.dot(a, b, preferred_element_type=F32)


def dot_nt(a, b):
    return lax.dot_general(a, b, NT, preferred_element_type=F32)


def kernel(
    g_in, c_in, out,
    base, recv, passing, both, green, vrecv, both2, coup, ccat, rights, acc, sig, wide,
    send_sem, recv_sem, local_sem,
):
    energy = lax.axis_index("energy")
    s = lax.axis_index("slab")
    g, z = energy // 8, energy % 8
    odd = g % 2
    mirror = g + 1 - 2 * odd
    lower_pair = g - 2 * (1 - odd)
    upper_pair = g + 2 * odd
    first, last = z == 0, z == 7
    edge = first | last
    zu, zd = (z + 1) % 8, (z + 7) % 8
    rows = [pl.ds(c * R, R) for c in range(N)]
    thick = [pl.ds(c * (B // NL), B // NL) for c in range(NL)]

    def piece(kind, c):
        return thick[c] if kind in (LOW, HIGH) else rows[c]

    def at(gg, zz):
        return (gg * 8 + zz, s)

    home = (energy, s)
    true = s >= 0
    up = (at(jnp.where(last, g, lower_pair), zu), last | (g >= 1))
    down = (at(jnp.where(first, g, upper_pair), zd), first | (g <= 6))
    vup = (at(jnp.where(last, g, mirror - 1), zu), last | (g != 1))
    vdown = (at(jnp.where(first, g, mirror + 1), zd), first | (g != 6))
    side_out = ((z == 1) & (g != 6)) | ((z == 6) & (g != 1))
    across = at(mirror, z)
    side_to = at(jnp.where(z == 1, mirror + 1, mirror - 1), jnp.where(z == 1, 0, 7))
    opposite = at(g, jnp.where(first, 7, 0))
    low_from = (at(jnp.where(first, g, mirror + 1), zd), first | (g != 6))
    high_from = (at(jnp.where(last, g, mirror - 1), zu), last | (g != 1))
    vlow_from = (at(jnp.where(first, g, upper_pair), zd), first | (g <= 6))
    vhigh_from = (at(jnp.where(last, g, lower_pair), zu), last | (g >= 1))
    slab_low, slab_high = ((energy, s - 1), s >= 1), ((energy, s + 1), s <= 6)
    side_in = (first & (g >= 1)) | (last & (g <= 6))

    def remote(kind, c, src, dst, dev, arrives):
        return pltpu.make_async_remote_copy(
            src_ref=src.at[piece(kind, c)], dst_ref=dst.at[piece(kind, c)],
            send_sem=send_sem.at[kind, c], recv_sem=recv_sem.at[arrives, c],
            device_id=dev, device_id_type=MESH,
        )

    def start(kind, c, src, dst, dev, cond, arrives=None):
        @pl.when(cond)
        def _():
            remote(kind, c, src, dst, dev, kind if arrives is None else arrives).start()

    def arrived(kind, c, dst, cond):
        @pl.when(cond)
        def _():
            remote(kind, c, dst, dst, home, kind).wait_recv()

    def sent(kind, c, src, cond):
        @pl.when(cond)
        def _():
            remote(kind, c, src, src, home, kind).wait_send()

    mir, own = base.at[0], base.at[1]

    loads = [
        pltpu.make_async_copy(g_in.at[0], base.at[1, :, pl.ds(0, B)], local_sem.at[0]),
        pltpu.make_async_copy(g_in.at[1], base.at[1, :, pl.ds(B, B)], local_sem.at[1]),
        pltpu.make_async_copy(c_in, coup, local_sem.at[2]),
    ]
    for load in loads:
        load.start()

    def flipped(zz):
        return jnp.where(z < 4, zz, 7 - zz)

    barrier = pltpu.get_barrier_semaphore()
    count = jnp.int32(1)
    for dev, cond in (
        low_from, high_from, vlow_from, vhigh_from, slab_low, slab_high,
        (across, true),
        *((at(g, flipped(source)), z == flipped(relay)) for source, _, relay in DETOURS),
        *((at(mirror, flipped(relay)), z == flipped(source)) for source, _, relay in DETOURS),
    ):
        @pl.when(cond)
        def _(dev=dev):
            pl.semaphore_signal(barrier, inc=1, device_id=dev, device_id_type=MESH)
    for cond in (
        up[1], down[1], vup[1], vdown[1], slab_low[1], slab_high[1],
        *(z == flipped(source) for source, _, _ in DETOURS),
        *(z == flipped(relay) for _, _, relay in DETOURS),
    ):
        count = count + cond.astype(jnp.int32)
    loads[0].wait()
    loads[1].wait()
    pl.semaphore_wait(barrier, count)

    def direct(c):
        cond = true
        for source, piece, _ in DETOURS:
            if piece == c:
                cond = cond & (z != flipped(source))
        return cond

    def detour(i):
        source, piece, relay = DETOURS[i]
        return pltpu.make_async_remote_copy(
            src_ref=own.at[rows[piece]], dst_ref=passing.at[i],
            send_sem=send_sem.at[RELAY, i], recv_sem=recv_sem.at[RELAY, i],
            device_id=at(g, flipped(relay)), device_id_type=MESH,
        )

    def onward(i):
        source, piece, relay = DETOURS[i]
        return pltpu.make_async_remote_copy(
            src_ref=passing.at[i], dst_ref=mir.at[rows[piece]],
            send_sem=send_sem.at[ONWARD, i], recv_sem=recv_sem.at[SWAP, piece],
            device_id=at(mirror, flipped(source)), device_id_type=MESH,
        )

    def swap(c):
        start(SWAP, c, own, mir, across, direct(c))

    for i, (source, _, _) in enumerate(DETOURS):
        @pl.when(z == flipped(source))
        def _(i=i):
            detour(i).start()
    for c in range(N):
        if c < WINDOW:
            swap(c)
        if c < NL:
            start(LOW, c, own, recv.at[0], *up)
            start(HIGH, c, own, recv.at[1], *down)

    def clear(ref, cond):
        @pl.when(cond)
        def _():
            ref[...] = jnp.zeros(ref.shape, ref.dtype)

    clear(recv.at[0], ~low_from[1])
    clear(recv.at[1], ~high_from[1])
    clear(recv.at[3], edge & ~side_in)
    clear(vrecv.at[0], ~vlow_from[1])
    clear(vrecv.at[1], ~vhigh_from[1])
    for target in (both.at[0], both.at[1], both2):
        clear(target.at[0], s == 0)
        clear(target.at[2], s == 7)

    loads[2].wait()
    for c in range(NC):
        for k in range(3):
            ccat[c, :, k * RC : (k + 1) * RC] = coup[k, :, c * RC : (c + 1) * RC]

    def widen(j, c):
        re = base[j, rows[c], 0:B]
        im = base[j, rows[c], B : 2 * B]
        wide[j, pl.ds(c * R, R), 0:B] = re
        wide[j, pl.ds(c * R, R), B : 2 * B] = -im
        wide[j, pl.ds(B + c * R, R), 0:B] = im
        wide[j, pl.ds(B + c * R, R), B : 2 * B] = re

    for c in range(N):
        widen(1, c)

    def add_up(target, a, b, c):
        target[1, rows[c]] = (a[rows[c]].astype(F32) + b[rows[c]].astype(F32)).astype(BF)

    def pass_halo(kind, c, target, cond=true):
        start(kind, c, target.at[1], target.at[2], slab_low[0], cond & slab_low[1])
        start(kind + 1, c, target.at[1], target.at[0], slab_high[0], cond & slab_high[1])

    def await_halo(kind, c, target):
        arrived(kind, c, target.at[2], slab_high[1])
        arrived(kind + 1, c, target.at[0], slab_low[1])

    def sigma_part(target, c, to):
        here = pl.ds(c * RC, RC)
        for k in range(3):
            stacked = jnp.concatenate([target[k, here, 0:B], target[k, here, B : 2 * B]], axis=0)
            right = dot_nt(stacked, coup[k]).astype(BF)
            rights[k * RC : (k + 1) * RC, 0:B] = right[0:RC]
            rights[k * RC : (k + 1) * RC, B : 2 * B] = right[RC : 2 * RC]
        part = dot(ccat[c], rights[...])
        if c == 0:
            to[...] = part
        else:
            to[...] += part

    def round_sigma(j):
        re = acc[j, :, 0:B].astype(BF)
        im = acc[j, :, B : 2 * B].astype(BF)
        sig[j, 0:B, 0:B] = re
        sig[j, 0:B, B : 2 * B] = im
        sig[j, B : 2 * B, 0:B] = -im
        sig[j, B : 2 * B, B : 2 * B] = re

    def result(j, lines):
        here = base[j, lines]
        prod = dot(here, sig[j]).astype(BF)
        return here.astype(F32) + dot_nt(prod, wide[j]) * (1.0 / B)

    def next_swap(c):
        if c + WINDOW < N:
            sent(SWAP, c, own, direct(c))
            swap(c + WINDOW)

    def forward(c):
        arrived(SWAP, c, mir, true)
        next_swap(c)

    for i, (_, _, relay) in enumerate(DETOURS):
        @pl.when(z == flipped(relay))
        def _(i=i):
            detour(i).wait_recv()
            onward(i).start()

    @pl.when(~edge)
    def _():
        for c in range(N + LAG):
            if c < N:
                if c % (N // NL) == 0:
                    arrived(LOW, c // (N // NL), recv.at[0], low_from[1])
                    arrived(HIGH, c // (N // NL), recv.at[1], high_from[1])
                add_up(both.at[0], recv.at[0], recv.at[1], c)
                pass_halo(HALO, c, both.at[0])
                forward(c)
                start(SIDE, c, mir, recv.at[3], side_to, side_out)
                widen(0, c)
            d = c - LAG
            if d >= 0:
                await_halo(HALO, d, both.at[0])
                if d % PER == PER - 1:
                    sigma_part(both.at[0], d // PER, acc.at[0])

    @pl.when(edge)
    def _():
        a0, b0 = jnp.where(first, 2, 0), jnp.where(last, 2, 1)
        a1, b1 = jnp.where(first, 0, 3), jnp.where(first, 3, 1)
        for c in range(N + LAG2):
            if c < N:
                forward(c)
                start(WRAP, c, mir, recv.at[2], opposite, true)
                widen(0, c)
            d = c - LAG1
            if 0 <= d < N:
                if d % (N // NL) == 0:
                    arrived(LOW, d // (N // NL), recv.at[0], low_from[1])
                    arrived(HIGH, d // (N // NL), recv.at[1], high_from[1])
                arrived(WRAP, d, recv.at[2], true)
                add_up(both.at[0], recv.at[a0], recv.at[b0], d)
                pass_halo(HALO, d, both.at[0])
                arrived(SIDE, d, recv.at[3], side_in)
                add_up(both.at[1], recv.at[a1], recv.at[b1], d)
                pass_halo(HALO + 2, d, both.at[1])
            d = c - LAG2
            if d >= 0:
                for j in range(2):
                    await_halo(HALO + 2 * j, d, both.at[j])
                    if d % PER == PER - 1:
                        sigma_part(both.at[j], d // PER, acc.at[j])
        round_sigma(1)

    round_sigma(0)
    for c in range(NC):
        @pl.when(edge)
        def _(c=c):
            green[1, pl.ds(c * RC, RC)] = result(1, pl.ds(c * RC, RC)).astype(BF)
            for d in range(c * PER, c * PER + PER):
                start(VLOW, d, green.at[1], vrecv.at[0], vup[0], last)
                start(VHIGH, d, green.at[1], vrecv.at[1], vdown[0], first)
        green[0, pl.ds(c * RC, RC)] = result(0, pl.ds(c * RC, RC)).astype(BF)
        for d in range(c * PER, c * PER + PER):
            start(VLOW, d, green.at[0], vrecv.at[0], vup[0], vup[1] & ~last)
            start(VHIGH, d, green.at[0], vrecv.at[1], vdown[0], vdown[1] & ~first)

    for c in range(N + PER):
        if c < N:
            arrived(VLOW, c, vrecv.at[0], vlow_from[1])
            arrived(VHIGH, c, vrecv.at[1], vhigh_from[1])
            add_up(both2, vrecv.at[0], vrecv.at[1], c)
            pass_halo(HALO2, c, both2)
        d = c - PER
        if d >= 0:
            await_halo(HALO2, d, both2)
            if d % PER == PER - 1:
                sigma_part(both2, d // PER, acc.at[1])
    round_sigma(1)
    final = result(1, slice(None)).astype(BF)
    for part in range(2):
        out[part] = final[:, part * B : part * B + B]

    for c in range(N):
        if c + WINDOW >= N:
            sent(SWAP, c, own, direct(c))
        if c < NL:
            sent(LOW, c, own, up[1])
            sent(HIGH, c, own, down[1])
        sent(WRAP, c, mir, edge)
        sent(SIDE, c, mir, side_out)
        for j in range(2):
            cond = true if j == 0 else edge
            sent(HALO + 2 * j, c, both.at[j, 1], cond & slab_low[1])
            sent(HALO + 2 * j + 1, c, both.at[j, 1], cond & slab_high[1])
        sent(VLOW, c, green.at[0], vup[1])
        sent(VHIGH, c, green.at[0], vdown[1])
        sent(HALO2, c, both2.at[1], slab_low[1])
        sent(HALO2 + 1, c, both2.at[1], slab_high[1])
    for i, (source, _, relay) in enumerate(DETOURS):
        @pl.when(z == flipped(source))
        def _(i=i):
            detour(i).wait_send()

        @pl.when(z == flipped(relay))
        def _(i=i):
            onward(i).wait_send()


def local(green0, coupling):
    block = (B, 2 * B)
    result = pl.pallas_call(
        kernel,
        out_shape=jax.ShapeDtypeStruct((2, B, B), BF),
        in_specs=[pl.BlockSpec(memory_space=pltpu.HBM)] * 2,
        out_specs=pl.BlockSpec(memory_space=pltpu.VMEM),
        scratch_shapes=[
            pltpu.VMEM((2, *block), BF),
            pltpu.VMEM((4, *block), BF),
            pltpu.VMEM((len(DETOURS), R, 2 * B), BF),
            pltpu.VMEM((2, 3, *block), BF),
            pltpu.VMEM((2, *block), BF),
            pltpu.VMEM((2, *block), BF),
            pltpu.VMEM((3, *block), BF),
            pltpu.VMEM((3, B, B), BF),
            pltpu.VMEM((NC, B, 3 * RC), BF),
            pltpu.VMEM((3 * RC, 2 * B), BF),
            pltpu.VMEM((2, *block), F32),
            pltpu.VMEM((2, 2 * B, 2 * B), BF),
            pltpu.VMEM((2, 2 * B, 2 * B), BF),
            pltpu.SemaphoreType.DMA((KINDS, N)),
            pltpu.SemaphoreType.DMA((KINDS, N)),
            pltpu.SemaphoreType.DMA((3,)),
        ],
        compiler_params=pltpu.CompilerParams(
            collective_id=0, has_side_effects=True, vmem_limit_bytes=53 * 1024 * 1024
        ),
        name="born",
    )(green0[0, 0], coupling[0])
    return result[None, None]


def solution(mesh):
    return jax.shard_map(
        local,
        mesh=mesh,
        in_specs=(P("energy", "slab", None, None, None), P("slab", None, None, None)),
        out_specs=P("energy", "slab", None, None, None),
        check_vma=False,
    )
```
